32 devices in a mesh: parts: 2 (over x), coord: 16 (over z, y, core).
Axes of the slice: x: 2, y: 2, z: 4, core: 2. Of those that a mesh axis runs over, the one named last changes fastest.
Arguments:
- shape_data: bfloat16 [128, 50, 6144], P('parts', None, 'coord'), parts along dimension 0, may hold values from -6 to 6
- frame_factor: bfloat16 [100, 16], P('parts'), parts along dimension 0, may hold values from -0.875 to 0.875
- coord_factor: bfloat16 [12288, 256], P(('parts', 'coord')), parts along dimension 0, may hold values from -0.078125 to 0.078125
- subject_factor: bfloat16 [128, 128], P(('parts', 'coord')), parts along dimension 0, may hold values from -6 to 6
Outputs:
- subject_update: float32 [128, 128], P(('parts', 'coord')), parts along dimension 0
The draws below stay inside these ranges and needn't reach their ends.
There are 2 independent parts, one for each index of `parts`. The reference program is written for one: setup_inputs(seed, part) draws one part's arguments, and reference() takes and returns one part's arrays. A program takes and returns all parts, laid end to end along the dimension named above; each array names one. Nothing has to cross between parts.
All inputs are finite; a program needn't handle non-finite values.
Results may differ from the reference program's by a relative error of at most 0.00088.
Values may be sent and summed in bfloat16 or wider, within the bound.
A program may use at most 64 MiB of HBM per device.

```python
import jax
import jax.numpy as jnp
from jax import lax

FRAMES = 50
R1 = 128
R2 = 16
R3 = 256
SUBJECTS = 64
COORDS = 6144


def strengthened(values, own_key, source, target, blocks, factor):
    def block_of(position):
        return (jnp.arange(values.shape[position]) // (values.shape[position] // blocks)).reshape((-1,) + (1,) * (values.ndim - 1 - position))

    first = jax.random.permutation(own_key, blocks)[block_of(target)]
    other_side = (block_of(target) + blocks // 2) % blocks
    return jnp.where((block_of(source) == first) | (block_of(source) == other_side), factor * values, values)


def level_of(own_key, dims, pieces, least, top_value):
    factor_of, own = 1.0, jax.random.fold_in(own_key, 6)
    for position, blocks in pieces:
        draws = jnp.exp(jax.random.uniform(jax.random.fold_in(own, position), (blocks,), jnp.float32, least / len(pieces), top_value / len(pieces)))
        factor_of = factor_of * jnp.repeat(draws, dims[position] // blocks).reshape([-1 if axis == position else 1 for axis in range(len(dims))])
    return factor_of


def centred(own_key, extent, deviation, bound, pieces=(), dtype=jnp.bfloat16):
    gain = level_of(own_key, extent, pieces, -0.22, 0.18) if pieces else 1.0
    drawn = jax.random.normal(own_key, extent, jnp.float32) * deviation * gain
    return jnp.minimum(jnp.maximum(drawn, -bound), bound).astype(dtype)


def noise_with(own_key, dims, scale, bound, cuts, heavy, kind=jnp.bfloat16):
    values = scale * jax.random.normal(own_key, dims, jnp.float32)
    if cuts:
        values = values * level_of(own_key, dims, cuts, -0.22, 0.18)
    return jnp.clip(strengthened(values, jax.random.fold_in(own_key, 3), *heavy), -bound, bound).astype(kind)


def setup_inputs(seed: int = 0, part: int = 0) -> dict:
    keys = jax.random.split(jax.random.key(seed), 5)
    part_keys = jax.random.split(jax.random.fold_in(keys[4], part), 5)
    return {
        "shape_data": noise_with(part_keys[0], (SUBJECTS, FRAMES, COORDS), 1.0, 6.0, ((2, 16),), (2, 0, 16, 2.0)),
        "frame_factor": centred(part_keys[1], (FRAMES, R2), FRAMES ** -0.5, 0.875),
        "coord_factor": centred(part_keys[2], (COORDS, R3), COORDS ** -0.5, 0.078125, ((0, 16),)),
        "subject_factor": centred(part_keys[3], (SUBJECTS, R1), 1.0, 6.0, ((0, 16),)),
    }


def reference(shape_data, frame_factor, coord_factor, subject_factor):
    subjects = shape_data.shape[0]
    mixed = jnp.einsum("sfc,fq->sqc", shape_data.astype(jnp.float32), frame_factor.astype(jnp.float32), precision=lax.Precision.HIGHEST)
    mixed = mixed.astype(jnp.bfloat16).reshape(subjects * R2, COORDS)
    core = jnp.dot(mixed, coord_factor, preferred_element_type=jnp.float32)
    core = core.reshape(subjects, R2 * R3).astype(jnp.bfloat16)
    gram = jnp.dot(core, core.T, preferred_element_type=jnp.float32) / (R2 * R3)
    return jnp.dot(gram, subject_factor.astype(jnp.float32), precision=lax.Precision.HIGHEST)
```

```python
import functools

import jax
import jax.numpy as jnp
from jax import lax
from jax.experimental import pallas as pl
from jax.experimental.pallas import tpu as pltpu
from jax.sharding import PartitionSpec as P

MESH = pl.DeviceIdType.MESH
F32 = jnp.float32
BF16 = jnp.bfloat16
GROUP = 16
CHUNKS = 4


def kernel(
    n,
    data_hbm,
    frame_hbm,
    coord_hbm,
    subject_hbm,
    out_ref,
    data,
    frame,
    coord,
    subject,
    own1,
    send1,
    recv1,
    own2,
    send2,
    recv2,
    send3,
    recv3,
    core_block,
    factor_slots,
    factor,
    update,
    update_send,
    update_recv,
    data_sem,
    small_sem,
    s1_sem,
    r1_sem,
    s2_sem,
    r2_sem,
    s3_sem,
    r3_sem,
    sf_sem,
    rf_sem,
    su_sem,
    ru_sem,
):
    part = lax.axis_index("parts")
    me = lax.axis_index("coord")
    core = lax.rem(me, 2)
    lo = lax.rem(lax.div(me, 2), 2)
    hi = lax.div(me, 4)
    nhi = n // 4
    frames, subjects, width = data.shape
    ranks_two = frame.shape[1]
    ranks_three = coord.shape[1]
    own_rows = subject.shape[0]
    rows = subjects // CHUNKS
    cols = ranks_two * ranks_three // n
    piece = min(cols, ranks_three)

    def remote(src, dst, send, recv, target):
        return pltpu.make_async_remote_copy(
            src_ref=src,
            dst_ref=dst,
            send_sem=send,
            recv_sem=recv,
            device_id=(part, target),
            device_id_type=MESH,
        )

    small = [
        pltpu.make_async_copy(frame_hbm, frame, small_sem.at[0]),
        pltpu.make_async_copy(coord_hbm, coord, small_sem.at[1]),
        pltpu.make_async_copy(subject_hbm, subject, small_sem.at[2]),
    ]
    loads = [
        pltpu.make_async_copy(
            data_hbm.at[:, pl.ds(k * rows, rows), :],
            data.at[:, pl.ds(k * rows, rows), :],
            data_sem.at[k],
        )
        for k in range(CHUNKS)
    ]
    small[0].start()
    loads[0].start()
    small[1].start()
    small[2].start()
    for k in range(1, CHUNKS):
        loads[k].start()

    barrier = pltpu.get_barrier_semaphore()
    for j in range(1, n):
        pl.semaphore_signal(
            barrier, inc=1, device_id=(part, lax.rem(me + j, n)), device_id_type=MESH
        )

    small[0].wait()
    tall = ranks_two * GROUP
    deep = frames * GROUP
    pick_q = (
        lax.broadcasted_iota(jnp.int32, (tall, ranks_two), 0) // GROUP
        == lax.broadcasted_iota(jnp.int32, (tall, ranks_two), 1)
    )
    pick_f = (
        lax.broadcasted_iota(jnp.int32, (frames, deep), 1) // GROUP
        == lax.broadcasted_iota(jnp.int32, (frames, deep), 0)
    )
    by_q = lax.dot_general(
        jnp.where(pick_q, 1.0, 0.0).astype(BF16),
        frame[...],
        (((1,), (1,)), ((), ())),
        preferred_element_type=F32,
    ).astype(BF16)
    spread = jnp.dot(by_q, jnp.where(pick_f, 1.0, 0.0).astype(BF16), preferred_element_type=F32)
    same = (
        lax.broadcasted_iota(jnp.int32, (tall, deep), 0) % GROUP
        == lax.broadcasted_iota(jnp.int32, (tall, deep), 1) % GROUP
    )
    weights = jnp.where(same, spread, 0.0).astype(BF16)

    small[1].wait()
    coord_value = coord[...]

    def compute(k):
        for g in range(rows // GROUP):
            first = k * rows + g * GROUP
            block = data[:, first : first + GROUP, :].reshape(deep, width)
            mixed = jnp.dot(weights, block, preferred_element_type=F32).astype(BF16)
            term = jnp.dot(mixed, coord_value, preferred_element_type=F32)
            pieces = {}
            for q in range(ranks_two):
                for b in range(ranks_three // piece):
                    start = q * ranks_three + b * piece
                    pieces[start // cols, start % cols] = term[
                        q * GROUP : (q + 1) * GROUP, b * piece : (b + 1) * piece
                    ]
            for (owner, at), zero in pieces.items():
                if owner % 2:
                    continue
                one = pieces[owner + 1, at]
                l, h = owner // 2 % 2, owner // 4
                own1[l, h, first : first + GROUP, at : at + piece] = jnp.where(core == 0, zero, one)
                send1[k, l, h, g * GROUP : (g + 1) * GROUP, at : at + piece] = jnp.where(
                    core == 0, one, zero
                ).astype(BF16)

    sends = []

    def begin(copy):
        copy.start()
        sends.append(copy)

    first_copies = [
        remote(send1.at[k], recv1.at[k], s1_sem.at[k], r1_sem.at[k], me + 1 - 2 * core)
        for k in range(CHUNKS)
    ]
    second_copies = [
        remote(send2.at[k], recv2.at[k], s2_sem.at[k], r2_sem.at[k], me + 2 - 4 * lo)
        for k in range(CHUNKS)
    ]
    third_copies = [
        [
            remote(
                send3.at[k, j - 1],
                recv3.at[k, j - 1],
                s3_sem.at[k, j - 1],
                r3_sem.at[k, j - 1],
                lax.rem(hi + j, nhi) * 4 + lo * 2 + core,
            )
            for j in range(1, nhi)
        ]
        for k in range(CHUNKS)
    ]
    factor_copies = [
        remote(
            factor_slots.at[me],
            factor_slots.at[me],
            sf_sem.at[j - 1],
            rf_sem.at[j - 1],
            lax.rem(me + j, n),
        )
        for j in range(1, n)
    ]
    update_copies = [
        remote(
            update_send.at[lax.rem(me + j, n)],
            update_recv.at[j - 1],
            su_sem.at[j - 1],
            ru_sem.at[j - 1],
            lax.rem(me + j, n),
        )
        for j in range(1, n)
    ]

    def second(k):
        first_copies[k].wait_recv()
        at = pl.ds(k * rows, rows)
        send2[k] = (own1[1 - lo, :, at, :] + recv1[k, 1 - lo].astype(F32)).astype(BF16)
        begin(second_copies[k])
        own2[:, at, :] = own1[lo, :, at, :] + recv1[k, lo].astype(F32)

    def third(k):
        second_copies[k].wait_recv()
        at = pl.ds(k * rows, rows)
        for j in range(1, nhi):
            there = lax.rem(hi + j, nhi)
            send3[k, j - 1] = (own2[there, at, :] + recv2[k, there].astype(F32)).astype(BF16)
            begin(third_copies[k][j - 1])

    def fourth(k):
        at = pl.ds(k * rows, rows)
        total = own2[hi, at, :] + recv2[k, hi].astype(F32)
        for j in range(1, nhi):
            third_copies[k][j - 1].wait_recv()
            total += recv3[k, j - 1].astype(F32)
        core_block[at, :] = total.astype(BF16)

    for step in range(CHUNKS + 2):
        if step < CHUNKS:
            loads[step].wait()
            compute(step)
            if step == 0:
                pl.semaphore_wait(barrier, n - 1)
            begin(first_copies[step])
        if 1 <= step <= CHUNKS:
            second(step - 1)
        if 2 <= step:
            third(step - 2)
        if step == 1:
            small[2].wait()
            factor_slots[me] = subject[...].astype(F32)
            for copy in factor_copies:
                begin(copy)
    for copy in factor_copies:
        copy.wait_recv()
    for d in range(n):
        factor[d * own_rows : (d + 1) * own_rows, :] = factor_slots[d]
    for k in range(CHUNKS):
        fourth(k)

    panel = core_block[...]
    gram = lax.dot_general(
        panel, panel, (((1,), (1,)), ((), ())), preferred_element_type=F32
    ) * (1.0 / (ranks_two * ranks_three))
    top = gram.astype(BF16)
    rest = gram - top.astype(F32)
    middle = rest.astype(BF16)
    low = (rest - middle.astype(F32)).astype(BF16)
    stacked = jnp.concatenate([top, middle, low], axis=0)
    product = jnp.dot(stacked, factor[...].astype(BF16), preferred_element_type=F32)
    update[...] = (
        product[:subjects] + (product[subjects : 2 * subjects] + product[2 * subjects :])
    )
    for d in range(n):
        update_send[d] = update[d * own_rows : (d + 1) * own_rows, :]
    for copy in update_copies:
        begin(copy)
    total = update_send[me]
    for j in range(1, n):
        update_copies[j - 1].wait_recv()
        total += update_recv[j - 1]
    out_ref[...] = total
    for copy in sends:
        copy.wait_send()


def body(shape_data, frame_factor, coord_factor, subject_factor):
    n = lax.axis_size("coord")
    subjects, frames, width = shape_data.shape
    ranks_two = frame_factor.shape[1]
    ranks_three = coord_factor.shape[1]
    own_rows, ranks_one = subject_factor.shape
    nhi = n // 4
    rows = subjects // CHUNKS
    cols = ranks_two * ranks_three // n
    dma = pltpu.SemaphoreType.DMA
    return pl.pallas_call(
        functools.partial(kernel, n),
        out_shape=jax.ShapeDtypeStruct((own_rows, ranks_one), F32),
        in_specs=[pl.BlockSpec(memory_space=pl.ANY)] * 4,
        out_specs=pl.BlockSpec(memory_space=pltpu.VMEM),
        scratch_shapes=[
            pltpu.VMEM((frames, subjects, width), BF16),
            pltpu.VMEM(frame_factor.shape, BF16),
            pltpu.VMEM(coord_factor.shape, BF16),
            pltpu.VMEM(subject_factor.shape, BF16),
            pltpu.VMEM((2, nhi, subjects, cols), F32),
            pltpu.VMEM((CHUNKS, 2, nhi, rows, cols), BF16),
            pltpu.VMEM((CHUNKS, 2, nhi, rows, cols), BF16),
            pltpu.VMEM((nhi, subjects, cols), F32),
            pltpu.VMEM((CHUNKS, nhi, rows, cols), BF16),
            pltpu.VMEM((CHUNKS, nhi, rows, cols), BF16),
            pltpu.VMEM((CHUNKS, nhi - 1, rows, cols), BF16),
            pltpu.VMEM((CHUNKS, nhi - 1, rows, cols), BF16),
            pltpu.VMEM((subjects, cols), BF16),
            pltpu.VMEM((n, own_rows, ranks_one), F32),
            pltpu.VMEM((subjects, ranks_one), F32),
            pltpu.VMEM((subjects, ranks_one), F32),
            pltpu.VMEM((n, own_rows, ranks_one), F32),
            pltpu.VMEM((n - 1, own_rows, ranks_one), F32),
            dma((CHUNKS,)),
            dma((3,)),
            dma((CHUNKS,)),
            dma((CHUNKS,)),
            dma((CHUNKS,)),
            dma((CHUNKS,)),
            dma((CHUNKS, nhi - 1)),
            dma((CHUNKS, nhi - 1)),
            dma((n - 1,)),
            dma((n - 1,)),
            dma((n - 1,)),
            dma((n - 1,)),
        ],
        compiler_params=pltpu.CompilerParams(
            collective_id=0, has_side_effects=True, vmem_limit_bytes=48 * 1024 * 1024
        ),
    )(jnp.transpose(shape_data, (1, 0, 2)), frame_factor, coord_factor, subject_factor)


def solution(mesh):
    in_specs = (
        P("parts", None, "coord"),
        P("parts", None),
        P(("parts", "coord"), None),
        P(("parts", "coord"), None),
    )
    out_specs = P(("parts", "coord"), None)
    return jax.shard_map(body, mesh=mesh, in_specs=in_specs, out_specs=out_specs, check_vma=False)
```

```python
import functools

import jax
import jax.numpy as jnp
from jax import lax
from jax.experimental import pallas as pl
from jax.experimental.pallas import tpu as pltpu
from jax.sharding import PartitionSpec as P

MESH = pl.DeviceIdType.MESH
F32 = jnp.float32
BF16 = jnp.bfloat16
GROUP = 16
LOADS = 4
CHUNKS = 2


def kernel(
    n,
    data_hbm,
    frame_hbm,
    coord_hbm,
    subject_hbm,
    out_ref,
    data,
    frame,
    coord,
    subject,
    own,
    send1,
    recv1,
    send2,
    recv2,
    core_block,
    factor_slots,
    factor,
    update,
    update_send,
    update_recv,
    data_sem,
    small_sem,
    s1_sem,
    r1_sem,
    s2_sem,
    r2_sem,
    sf_sem,
    rf_sem,
    su_sem,
    ru_sem,
):
    part = lax.axis_index("parts")
    me = lax.axis_index("coord")
    core = lax.rem(me, 2)
    chip = lax.div(me, 2)
    chips = n // 2
    frames, subjects, width = data.shape
    ranks_two = frame.shape[0]
    ranks_three = coord.shape[1]
    own_rows = subject.shape[0]
    load_rows = subjects // LOADS
    rows = subjects // CHUNKS
    cols = ranks_two * ranks_three // n
    piece = min(cols, ranks_three)

    def partner(index, mask):
        bit = 1
        while bit <= mask:
            if mask & bit:
                index = index + bit - 2 * bit * lax.rem(lax.div(index, bit), 2)
            bit *= 2
        return index

    def remote(src, dst, send, recv, target):
        return pltpu.make_async_remote_copy(
            src_ref=src,
            dst_ref=dst,
            send_sem=send,
            recv_sem=recv,
            device_id=(part, target),
            device_id_type=MESH,
        )

    barrier = pltpu.get_barrier_semaphore()
    for mask in range(n - 1, 0, -1):
        pl.semaphore_signal(
            barrier, inc=1, device_id=(part, partner(me, mask)), device_id_type=MESH
        )

    small = [
        pltpu.make_async_copy(frame_hbm, frame, small_sem.at[0]),
        pltpu.make_async_copy(coord_hbm, coord, small_sem.at[1]),
        pltpu.make_async_copy(subject_hbm, subject, small_sem.at[2]),
    ]
    loads = [
        pltpu.make_async_copy(
            data_hbm.at[:, pl.ds(k * load_rows, load_rows), :],
            data.at[:, pl.ds(k * load_rows, load_rows), :],
            data_sem.at[k],
        )
        for k in range(LOADS)
    ]
    small[0].start()
    loads[0].start()
    small[1].start()
    small[2].start()
    for k in range(1, LOADS):
        loads[k].start()

    small[0].wait()
    tall = ranks_two * GROUP
    deep = frames * GROUP
    pick_q = (
        lax.broadcasted_iota(jnp.int32, (tall, ranks_two), 0) // GROUP
        == lax.broadcasted_iota(jnp.int32, (tall, ranks_two), 1)
    )
    pick_f = (
        lax.broadcasted_iota(jnp.int32, (frames, deep), 1) // GROUP
        == lax.broadcasted_iota(jnp.int32, (frames, deep), 0)
    )
    by_q = jnp.dot(
        jnp.where(pick_q, 1.0, 0.0).astype(BF16), frame[...], preferred_element_type=F32
    ).astype(BF16)
    spread = jnp.dot(by_q, jnp.where(pick_f, 1.0, 0.0).astype(BF16), preferred_element_type=F32)
    same = (
        lax.broadcasted_iota(jnp.int32, (tall, deep), 0) % GROUP
        == lax.broadcasted_iota(jnp.int32, (tall, deep), 1) % GROUP
    )
    weights = jnp.where(same, spread, 0.0).astype(BF16)

    small[1].wait()
    coord_value = coord[...]

    def compute(first):
        block = data[:, first : first + GROUP, :].reshape(deep, width)
        mixed = jnp.dot(weights, block, preferred_element_type=F32).astype(BF16)
        term = jnp.dot(mixed, coord_value, preferred_element_type=F32)
        pieces = {}
        for q in range(ranks_two):
            for b in range(ranks_three // piece):
                start = q * ranks_three + b * piece
                pieces[start // cols, start % cols] = term[
                    q * GROUP : (q + 1) * GROUP, b * piece : (b + 1) * piece
                ]
        chunk, at = first // rows, first % rows
        for (owner, left), zero in pieces.items():
            if owner % 2:
                continue
            one = pieces[owner + 1, left]
            own[owner // 2, first : first + GROUP, left : left + piece] = jnp.where(
                core == 0, zero, one
            )
            send1[chunk, owner // 2, at : at + GROUP, left : left + piece] = jnp.where(
                core == 0, one, zero
            ).astype(send1.dtype)

    sends = []

    def begin(copy):
        copy.start()
        sends.append(copy)

    sibling_copies = [
        remote(send1.at[k], recv1.at[k], s1_sem.at[k], r1_sem.at[k], partner(me, 1))
        for k in range(CHUNKS)
    ]
    chip_copies = [
        {
            mask: remote(
                send2.at[k, mask - 1],
                recv2.at[k, mask - 1],
                s2_sem.at[k, mask - 1],
                r2_sem.at[k, mask - 1],
                partner(me, 2 * mask),
            )
            for mask in range(chips - 1, 0, -1)
        }
        for k in range(CHUNKS)
    ]
    factor_copies = [
        remote(
            factor_slots.at[me],
            factor_slots.at[me],
            sf_sem.at[mask - 1],
            rf_sem.at[mask - 1],
            partner(me, mask),
        )
        for mask in range(n - 1, 0, -1)
    ]
    update_copies = [
        remote(
            update_send.at[partner(me, mask)],
            update_recv.at[mask - 1],
            su_sem.at[mask - 1],
            ru_sem.at[mask - 1],
            partner(me, mask),
        )
        for mask in range(n - 1, 0, -1)
    ]

    for first in range(0, subjects, GROUP):
        if first % load_rows == 0:
            loads[first // load_rows].wait()
        compute(first)
    small[2].wait()
    factor_slots[me] = subject[...].astype(F32)

    pl.semaphore_wait(barrier, n - 1)
    for copy in sibling_copies:
        begin(copy)
    for k in range(CHUNKS):
        sibling_copies[k].wait_recv()
        at = pl.ds(k * rows, rows)
        for mask, copy in chip_copies[k].items():
            there = partner(chip, mask)
            send2[k, mask - 1] = (own[there, at, :] + recv1[k, there].astype(F32)).astype(BF16)
            begin(copy)
    for copy in factor_copies:
        begin(copy)
    for copy in factor_copies:
        copy.wait_recv()
    for d in range(n):
        factor[d * own_rows : (d + 1) * own_rows, :] = factor_slots[d]
    for k in range(CHUNKS):
        at = pl.ds(k * rows, rows)
        total = own[chip, at, :] + recv1[k, chip].astype(F32)
        for mask in range(1, chips):
            chip_copies[k][mask].wait_recv()
            total += recv2[k, mask - 1].astype(F32)
        core_block[at, :] = total.astype(BF16)

    panel = core_block[...]
    gram = lax.dot_general(
        panel, panel, (((1,), (1,)), ((), ())), preferred_element_type=F32
    ) * (1.0 / (ranks_two * ranks_three))
    top = gram.astype(BF16)
    rest = gram - top.astype(F32)
    middle = rest.astype(BF16)
    low = (rest - middle.astype(F32)).astype(BF16)
    stacked = jnp.concatenate([top, middle, low], axis=0)
    product = jnp.dot(stacked, factor[...].astype(BF16), preferred_element_type=F32)
    update[...] = (
        product[:subjects] + (product[subjects : 2 * subjects] + product[2 * subjects :])
    )
    for d in range(n):
        update_send[d] = update[d * own_rows : (d + 1) * own_rows, :]
    for copy in update_copies:
        begin(copy)
    total = update_send[me]
    for copy in reversed(update_copies):
        copy.wait_recv()
    for mask in range(1, n):
        total += update_recv[mask - 1]
    out_ref[...] = total
    for copy in sends:
        copy.wait_send()


def body(shape_data, frame_factor, coord_factor, subject_factor):
    n = lax.axis_size("coord")
    subjects, frames, width = shape_data.shape
    ranks_two = frame_factor.shape[1]
    ranks_three = coord_factor.shape[1]
    own_rows, ranks_one = subject_factor.shape
    chips = n // 2
    rows = subjects // CHUNKS
    cols = ranks_two * ranks_three // n
    dma = pltpu.SemaphoreType.DMA
    return pl.pallas_call(
        functools.partial(kernel, n),
        out_shape=jax.ShapeDtypeStruct((own_rows, ranks_one), F32),
        in_specs=[pl.BlockSpec(memory_space=pl.ANY)] * 4,
        out_specs=pl.BlockSpec(memory_space=pltpu.VMEM),
        scratch_shapes=[
            pltpu.VMEM((frames, subjects, width), BF16),
            pltpu.VMEM((ranks_two, frames), BF16),
            pltpu.VMEM(coord_factor.shape, BF16),
            pltpu.VMEM(subject_factor.shape, BF16),
            pltpu.VMEM((chips, subjects, cols), F32),
            pltpu.VMEM((CHUNKS, chips, rows, cols), BF16),
            pltpu.VMEM((CHUNKS, chips, rows, cols), BF16),
            pltpu.VMEM((CHUNKS, chips - 1, rows, cols), BF16),
            pltpu.VMEM((CHUNKS, chips - 1, rows, cols), BF16),
            pltpu.VMEM((subjects, cols), BF16),
            pltpu.VMEM((n, own_rows, ranks_one), F32),
            pltpu.VMEM((subjects, ranks_one), F32),
            pltpu.VMEM((subjects, ranks_one), F32),
            pltpu.VMEM((n, own_rows, ranks_one), F32),
            pltpu.VMEM((n - 1, own_rows, ranks_one), F32),
            dma((LOADS,)),
            dma((3,)),
            dma((CHUNKS,)),
            dma((CHUNKS,)),
            dma((CHUNKS, chips - 1)),
            dma((CHUNKS, chips - 1)),
            dma((n - 1,)),
            dma((n - 1,)),
            dma((n - 1,)),
            dma((n - 1,)),
        ],
        compiler_params=pltpu.CompilerParams(
            collective_id=0, has_side_effects=True, vmem_limit_bytes=60 * 1024 * 1024
        ),
    )(jnp.transpose(shape_data, (1, 0, 2)), frame_factor.T, coord_factor, subject_factor)


def solution(mesh):
    in_specs = (
        P("parts", None, "coord"),
        P("parts", None),
        P(("parts", "coord"), None),
        P(("parts", "coord"), None),
    )
    out_specs = P(("parts", "coord"), None)
    return jax.shard_map(body, mesh=mesh, in_specs=in_specs, out_specs=out_specs, check_vma=False)
```

```python
import functools

import jax
import jax.numpy as jnp
from jax import lax
from jax.experimental import pallas as pl
from jax.experimental.pallas import tpu as pltpu
from jax.sharding import PartitionSpec as P

MESH = pl.DeviceIdType.MESH
F32 = jnp.float32
BF16 = jnp.bfloat16
GROUP = 16
LOADS = 4
CHUNKS = 2


def kernel(
    n,
    data_hbm,
    frame_hbm,
    coord_hbm,
    subject_hbm,
    out_ref,
    data,
    frame,
    coord,
    subject,
    own,
    send1,
    recv1,
    y_send_first,
    y_recv_first,
    z_send_first,
    z_recv_first,
    y_send_last,
    y_recv_last,
    z_send_last,
    z_recv_last,
    core_block,
    factor_slots,
    factor,
    update,
    update_send,
    update_recv,
    data_sem,
    small_sem,
    s1_sem,
    r1_sem,
    sy_sem,
    ry_sem,
    sz_sem,
    rz_sem,
    sf_sem,
    rf_sem,
    su_sem,
    ru_sem,
):
    part = lax.axis_index("parts")
    me = lax.axis_index("coord")
    core = lax.rem(me, 2)
    lo = lax.rem(lax.div(me, 2), 2)
    hi = lax.div(me, 4)
    nhi = n // 4
    frames, subjects, width = data.shape
    ranks_two = frame.shape[0]
    ranks_three = coord.shape[1]
    own_rows = subject.shape[0]
    load_rows = subjects // LOADS
    rows = subjects // CHUNKS
    cols = ranks_two * ranks_three // n
    piece = min(cols, ranks_three)

    def partner(index, mask):
        bit = 1
        while bit <= mask:
            if mask & bit:
                index = index + bit - 2 * bit * lax.rem(lax.div(index, bit), 2)
            bit *= 2
        return index

    def remote(src, dst, send, recv, target):
        return pltpu.make_async_remote_copy(
            src_ref=src,
            dst_ref=dst,
            send_sem=send,
            recv_sem=recv,
            device_id=(part, target),
            device_id_type=MESH,
        )

    barrier = pltpu.get_barrier_semaphore()
    partners = [4 * mask for mask in range(nhi - 1, 0, -1)] + [2, 1]
    for mask in partners:
        pl.semaphore_signal(
            barrier, inc=1, device_id=(part, partner(me, mask)), device_id_type=MESH
        )

    small = [
        pltpu.make_async_copy(frame_hbm, frame, small_sem.at[0]),
        pltpu.make_async_copy(coord_hbm, coord, small_sem.at[1]),
        pltpu.make_async_copy(subject_hbm, subject, small_sem.at[2]),
    ]
    loads = [
        pltpu.make_async_copy(
            data_hbm.at[:, pl.ds(k * load_rows, load_rows), :],
            data.at[:, pl.ds(k * load_rows, load_rows), :],
            data_sem.at[k],
        )
        for k in range(LOADS)
    ]
    small[0].start()
    loads[0].start()
    small[1].start()
    small[2].start()
    for k in range(1, LOADS):
        loads[k].start()

    small[0].wait()
    tall = ranks_two * GROUP
    deep = frames * GROUP
    pick_q = (
        lax.broadcasted_iota(jnp.int32, (tall, ranks_two), 0) // GROUP
        == lax.broadcasted_iota(jnp.int32, (tall, ranks_two), 1)
    )
    pick_f = (
        lax.broadcasted_iota(jnp.int32, (frames, deep), 1) // GROUP
        == lax.broadcasted_iota(jnp.int32, (frames, deep), 0)
    )
    by_q = jnp.dot(
        jnp.where(pick_q, 1.0, 0.0).astype(BF16), frame[...], preferred_element_type=F32
    ).astype(BF16)
    spread = jnp.dot(by_q, jnp.where(pick_f, 1.0, 0.0).astype(BF16), preferred_element_type=F32)
    same = (
        lax.broadcasted_iota(jnp.int32, (tall, deep), 0) % GROUP
        == lax.broadcasted_iota(jnp.int32, (tall, deep), 1) % GROUP
    )
    weights = jnp.where(same, spread, 0.0).astype(BF16)

    small[1].wait()
    coord_value = coord[...]

    def compute(first):
        block = data[:, first : first + GROUP, :].reshape(deep, width)
        mixed = jnp.dot(weights, block, preferred_element_type=F32).astype(BF16)
        term = jnp.dot(mixed, coord_value, preferred_element_type=F32)
        pieces = {}
        for q in range(ranks_two):
            for b in range(ranks_three // piece):
                start = q * ranks_three + b * piece
                pieces[start // cols, start % cols] = term[
                    q * GROUP : (q + 1) * GROUP, b * piece : (b + 1) * piece
                ]
        chunk, at = first // rows, first % rows
        for (owner, left), zero in pieces.items():
            if owner % 2:
                continue
            one = pieces[owner + 1, left]
            low, high = owner // 2 % 2, owner // 4
            own[low, high, first : first + GROUP, left : left + piece] = jnp.where(
                core == 0, zero, one
            )
            send1[chunk, low, high, at : at + GROUP, left : left + piece] = jnp.where(
                core == 0, one, zero
            ).astype(send1.dtype)

    sends = []

    def begin(copy):
        copy.start()
        sends.append(copy)

    sibling_copies = [
        remote(send1.at[k], recv1.at[k], s1_sem.at[k], r1_sem.at[k], partner(me, 1))
        for k in range(CHUNKS)
    ]
    z_masks = range(nhi - 1, 0, -1)
    y_first = remote(y_send_first, y_recv_first, sy_sem.at[0], ry_sem.at[0], partner(me, 2))
    y_last = remote(y_send_last, y_recv_last, sy_sem.at[1], ry_sem.at[1], partner(me, 2))
    z_first = {
        mask: remote(
            z_send_first.at[mask - 1],
            z_recv_first.at[mask - 1],
            sz_sem.at[0, mask - 1],
            rz_sem.at[0, mask - 1],
            partner(me, 4 * mask),
        )
        for mask in z_masks
    }
    z_last = {
        mask: remote(
            z_send_last.at[mask - 1],
            z_recv_last.at[mask - 1],
            sz_sem.at[1, mask - 1],
            rz_sem.at[1, mask - 1],
            partner(me, 4 * mask),
        )
        for mask in z_masks
    }

    def factor_copy(start, count, sem, target):
        slots = factor_slots.at[pl.ds(start, count)]
        return remote(slots, slots, sf_sem.at[sem], rf_sem.at[sem], target)

    factor_sibling = factor_copy(me, 1, 0, partner(me, 1))
    factor_y = factor_copy(me - core, 2, 1, partner(me, 2))
    factor_z = [
        factor_copy(hi * 4, 4, 1 + mask, partner(me, 4 * mask)) for mask in z_masks
    ]
    update_copies = [
        remote(
            update_send.at[partner(me, mask)],
            update_recv.at[mask - 1],
            su_sem.at[mask - 1],
            ru_sem.at[mask - 1],
            partner(me, mask),
        )
        for mask in range(n - 1, 0, -1)
    ]

    for first in range(0, subjects, GROUP):
        if first % load_rows == 0:
            loads[first // load_rows].wait()
        compute(first)
    small[2].wait()
    factor_slots[me] = subject[...].astype(F32)

    pl.semaphore_wait(barrier, len(partners))
    for copy in sibling_copies:
        begin(copy)
    begin(factor_sibling)
    a = pl.ds(0, rows)
    b = pl.ds(rows, rows)

    sibling_copies[0].wait_recv()
    y_send_first[...] = (own[1 - lo, :, a, :] + recv1[0, 1 - lo].astype(F32)).astype(BF16)
    begin(y_first)
    sibling_copies[1].wait_recv()
    for mask in z_masks:
        there = partner(hi, mask)
        z_send_first[mask - 1] = (own[:, there, b, :] + recv1[1, :, there].astype(F32)).astype(BF16)
        begin(z_first[mask])
    factor_sibling.wait_recv()
    begin(factor_y)
    own[lo, :, a, :] = own[lo, :, a, :] + recv1[0, lo].astype(F32)
    own[:, hi, b, :] = own[:, hi, b, :] + recv1[1, :, hi].astype(F32)

    y_first.wait_recv()
    for mask in z_masks:
        there = partner(hi, mask)
        z_send_last[mask - 1] = (own[lo, there, a, :] + y_recv_first[there].astype(F32)).astype(BF16)
        begin(z_last[mask])
    factor_y.wait_recv()
    for copy in factor_z:
        begin(copy)
    for mask in reversed(z_masks):
        z_first[mask].wait_recv()
    total = own[1 - lo, hi, b, :]
    for mask in z_masks:
        total += z_recv_first[mask - 1, 1 - lo].astype(F32)
    y_send_last[...] = total.astype(BF16)
    begin(y_last)
    total_a = own[lo, hi, a, :] + y_recv_first[hi].astype(F32)
    total_b = own[lo, hi, b, :]
    for mask in z_masks:
        total_b += z_recv_first[mask - 1, lo].astype(F32)
    for copy in factor_z:
        copy.wait_recv()
    for d in range(n):
        factor[d * own_rows : (d + 1) * own_rows, :] = factor_slots[d]
    for mask in reversed(z_masks):
        z_last[mask].wait_recv()
        total_a += z_recv_last[mask - 1].astype(F32)
    core_block[a, :] = total_a.astype(BF16)
    y_last.wait_recv()
    core_block[b, :] = (total_b + y_recv_last[...].astype(F32)).astype(BF16)

    panel = core_block[...]
    gram = lax.dot_general(
        panel, panel, (((1,), (1,)), ((), ())), preferred_element_type=F32
    ) * (1.0 / (ranks_two * ranks_three))
    top = gram.astype(BF16)
    rest = gram - top.astype(F32)
    middle = rest.astype(BF16)
    low = (rest - middle.astype(F32)).astype(BF16)
    stacked = jnp.concatenate([top, middle, low], axis=0)
    product = jnp.dot(stacked, factor[...].astype(BF16), preferred_element_type=F32)
    update[...] = (
        product[:subjects] + (product[subjects : 2 * subjects] + product[2 * subjects :])
    )
    for d in range(n):
        update_send[d] = update[d * own_rows : (d + 1) * own_rows, :]
    for copy in update_copies:
        begin(copy)
    total = update_send[me]
    for copy in reversed(update_copies):
        copy.wait_recv()
    for mask in range(1, n):
        total += update_recv[mask - 1]
    out_ref[...] = total
    for copy in sends:
        copy.wait_send()


def body(shape_data, frame_factor, coord_factor, subject_factor):
    n = lax.axis_size("coord")
    subjects, frames, width = shape_data.shape
    ranks_two = frame_factor.shape[1]
    ranks_three = coord_factor.shape[1]
    own_rows, ranks_one = subject_factor.shape
    nhi = n // 4
    rows = subjects // CHUNKS
    cols = ranks_two * ranks_three // n
    dma = pltpu.SemaphoreType.DMA
    return pl.pallas_call(
        functools.partial(kernel, n),
        out_shape=jax.ShapeDtypeStruct((own_rows, ranks_one), F32),
        in_specs=[pl.BlockSpec(memory_space=pl.ANY)] * 4,
        out_specs=pl.BlockSpec(memory_space=pltpu.VMEM),
        scratch_shapes=[
            pltpu.VMEM((frames, subjects, width), BF16),
            pltpu.VMEM((ranks_two, frames), BF16),
            pltpu.VMEM(coord_factor.shape, BF16),
            pltpu.VMEM(subject_factor.shape, BF16),
            pltpu.VMEM((2, nhi, subjects, cols), F32),
            pltpu.VMEM((CHUNKS, 2, nhi, rows, cols), BF16),
            pltpu.VMEM((CHUNKS, 2, nhi, rows, cols), BF16),
            pltpu.VMEM((nhi, rows, cols), BF16),
            pltpu.VMEM((nhi, rows, cols), BF16),
            pltpu.VMEM((nhi - 1, 2, rows, cols), BF16),
            pltpu.VMEM((nhi - 1, 2, rows, cols), BF16),
            pltpu.VMEM((rows, cols), BF16),
            pltpu.VMEM((rows, cols), BF16),
            pltpu.VMEM((nhi - 1, rows, cols), BF16),
            pltpu.VMEM((nhi - 1, rows, cols), BF16),
            pltpu.VMEM((subjects, cols), BF16),
            pltpu.VMEM((n, own_rows, ranks_one), F32),
            pltpu.VMEM((subjects, ranks_one), F32),
            pltpu.VMEM((subjects, ranks_one), F32),
            pltpu.VMEM((n, own_rows, ranks_one), F32),
            pltpu.VMEM((n - 1, own_rows, ranks_one), F32),
            dma((LOADS,)),
            dma((3,)),
            dma((CHUNKS,)),
            dma((CHUNKS,)),
            dma((2,)),
            dma((2,)),
            dma((2, nhi - 1)),
            dma((2, nhi - 1)),
            dma((1 + nhi,)),
            dma((1 + nhi,)),
            dma((n - 1,)),
            dma((n - 1,)),
        ],
        compiler_params=pltpu.CompilerParams(
            collective_id=0, has_side_effects=True, vmem_limit_bytes=60 * 1024 * 1024
        ),
    )(jnp.transpose(shape_data, (1, 0, 2)), frame_factor.T, coord_factor, subject_factor)


def solution(mesh):
    in_specs = (
        P("parts", None, "coord"),
        P("parts", None),
        P(("parts", "coord"), None),
        P(("parts", "coord"), None),
    )
    out_specs = P(("parts", "coord"), None)
    return jax.shard_map(body, mesh=mesh, in_specs=in_specs, out_specs=out_specs, check_vma=False)
```

```python
import functools

import jax
import jax.numpy as jnp
from jax import lax
from jax.experimental import pallas as pl
from jax.experimental.pallas import tpu as pltpu
from jax.sharding import PartitionSpec as P

MESH = pl.DeviceIdType.MESH
F32 = jnp.float32
BF16 = jnp.bfloat16
GROUP = 16
LOADS = 2
CHUNKS = 2


def kernel(
    n,
    data_hbm,
    frame_hbm,
    coord_hbm,
    subject_hbm,
    out_ref,
    data,
    frame,
    coord,
    subject,
    own,
    send1,
    recv1,
    y_send_first,
    y_recv_first,
    z_send_first,
    z_recv_first,
    y_send_last,
    y_recv_last,
    z_send_last,
    z_recv_last,
    core_block,
    factor_slots,
    factor,
    update,
    update_send,
    update_recv,
    data_sem,
    small_sem,
    s1_sem,
    r1_sem,
    sy_sem,
    ry_sem,
    sz_sem,
    rz_sem,
    sf_sem,
    rf_sem,
    su_sem,
    ru_sem,
):
    part = lax.axis_index("parts")
    me = lax.axis_index("coord")
    core = lax.rem(me, 2)
    lo = lax.rem(lax.div(me, 2), 2)
    hi = lax.div(me, 4)
    nhi = n // 4
    frames, subjects, width = data.shape
    ranks_two = frame.shape[0]
    ranks_three = coord.shape[1]
    own_rows = subject.shape[0]
    load_rows = subjects // LOADS
    rows = subjects // CHUNKS
    cols = ranks_two * ranks_three // n
    piece = min(cols, ranks_three)

    def partner(index, mask):
        bit = 1
        while bit <= mask:
            if mask & bit:
                index = index + bit - 2 * bit * lax.rem(lax.div(index, bit), 2)
            bit *= 2
        return index

    def remote(src, dst, send, recv, target):
        return pltpu.make_async_remote_copy(
            src_ref=src,
            dst_ref=dst,
            send_sem=send,
            recv_sem=recv,
            device_id=(part, target),
            device_id_type=MESH,
        )

    barrier = pltpu.get_barrier_semaphore()
    partners = [4 * mask for mask in range(nhi - 1, 0, -1)] + [2, 1]
    for mask in partners:
        pl.semaphore_signal(
            barrier, inc=1, device_id=(part, partner(me, mask)), device_id_type=MESH
        )

    small = [
        pltpu.make_async_copy(frame_hbm, frame, small_sem.at[0]),
        pltpu.make_async_copy(coord_hbm, coord, small_sem.at[1]),
        pltpu.make_async_copy(subject_hbm, subject, small_sem.at[2]),
    ]
    loads = [
        pltpu.make_async_copy(
            data_hbm.at[:, pl.ds(k * load_rows, load_rows), :],
            data.at[:, pl.ds(k * load_rows, load_rows), :],
            data_sem.at[k],
        )
        for k in range(LOADS)
    ]
    small[0].start()
    loads[0].start()
    small[1].start()
    small[2].start()
    for k in range(1, LOADS):
        loads[k].start()

    small[0].wait()
    tall = ranks_two * GROUP
    deep = frames * GROUP
    pick_q = (
        lax.broadcasted_iota(jnp.int32, (tall, ranks_two), 0) // GROUP
        == lax.broadcasted_iota(jnp.int32, (tall, ranks_two), 1)
    )
    pick_f = (
        lax.broadcasted_iota(jnp.int32, (frames, deep), 1) // GROUP
        == lax.broadcasted_iota(jnp.int32, (frames, deep), 0)
    )
    by_q = jnp.dot(
        jnp.where(pick_q, 1.0, 0.0).astype(BF16), frame[...], preferred_element_type=F32
    ).astype(BF16)
    spread = jnp.dot(by_q, jnp.where(pick_f, 1.0, 0.0).astype(BF16), preferred_element_type=F32)
    same = (
        lax.broadcasted_iota(jnp.int32, (tall, deep), 0) % GROUP
        == lax.broadcasted_iota(jnp.int32, (tall, deep), 1) % GROUP
    )
    weights = jnp.where(same, spread, 0.0).astype(BF16)

    small[1].wait()
    coord_value = coord[...]

    def mix(first):
        block = data[:, first : first + GROUP, :].reshape(deep, width)
        return jnp.dot(weights, block, preferred_element_type=F32).astype(BF16)

    def compute(first, mixed):
        term = jnp.dot(mixed, coord_value, preferred_element_type=F32)
        pieces = {}
        for q in range(ranks_two):
            for b in range(ranks_three // piece):
                start = q * ranks_three + b * piece
                pieces[start // cols, start % cols] = term[
                    q * GROUP : (q + 1) * GROUP, b * piece : (b + 1) * piece
                ]
        chunk, at = first // rows, first % rows
        for (owner, left), zero in pieces.items():
            if owner % 2:
                continue
            one = pieces[owner + 1, left]
            low, high = owner // 2 % 2, owner // 4
            own[low, high, first : first + GROUP, left : left + piece] = jnp.where(
                core == 0, zero, one
            )
            send1[chunk, low, high, at : at + GROUP, left : left + piece] = jnp.where(
                core == 0, one, zero
            ).astype(send1.dtype)

    sends = []

    def begin(copy):
        copy.start()
        sends.append(copy)

    sibling_copies = [
        remote(send1.at[k], recv1.at[k], s1_sem.at[k], r1_sem.at[k], partner(me, 1))
        for k in range(CHUNKS)
    ]
    z_masks = range(nhi - 1, 0, -1)
    y_first = remote(y_send_first, y_recv_first, sy_sem.at[0], ry_sem.at[0], partner(me, 2))
    y_last = remote(y_send_last, y_recv_last, sy_sem.at[1], ry_sem.at[1], partner(me, 2))
    z_first = {
        mask: remote(
            z_send_first.at[mask - 1],
            z_recv_first.at[mask - 1],
            sz_sem.at[0, mask - 1],
            rz_sem.at[0, mask - 1],
            partner(me, 4 * mask),
        )
        for mask in z_masks
    }
    z_last = {
        mask: remote(
            z_send_last.at[mask - 1],
            z_recv_last.at[mask - 1],
            sz_sem.at[1, mask - 1],
            rz_sem.at[1, mask - 1],
            partner(me, 4 * mask),
        )
        for mask in z_masks
    }

    def factor_copy(start, count, sem, target):
        slots = factor_slots.at[pl.ds(start, count)]
        return remote(slots, slots, sf_sem.at[sem], rf_sem.at[sem], target)

    factor_sibling = factor_copy(me, 1, 0, partner(me, 1))
    factor_y = factor_copy(me - core, 2, 1, partner(me, 2))
    factor_z = [
        factor_copy(hi * 4, 4, 1 + mask, partner(me, 4 * mask)) for mask in z_masks
    ]
    update_copies = [
        remote(
            update_send.at[partner(me, mask)],
            update_recv.at[mask - 1],
            su_sem.at[mask - 1],
            ru_sem.at[mask - 1],
            partner(me, mask),
        )
        for mask in range(n - 1, 0, -1)
    ]

    small[2].wait()
    factor_slots[me] = subject[...].astype(F32)
    mixed = []
    for first in range(0, subjects, GROUP):
        if first % load_rows == 0:
            loads[first // load_rows].wait()
        mixed.append((first, mix(first)))
        if (first + GROUP) % rows == 0:
            for item in mixed:
                compute(*item)
            mixed = []
        if first + GROUP == rows:
            pl.semaphore_wait(barrier, len(partners))
            begin(sibling_copies[0])
            begin(factor_sibling)
    begin(sibling_copies[1])
    a = pl.ds(0, rows)
    b = pl.ds(rows, rows)

    sibling_copies[0].wait_recv()
    y_send_first[...] = (own[1 - lo, :, a, :] + recv1[0, 1 - lo].astype(F32)).astype(BF16)
    begin(y_first)
    sibling_copies[1].wait_recv()
    for mask in z_masks:
        there = partner(hi, mask)
        z_send_first[mask - 1] = (own[:, there, b, :] + recv1[1, :, there].astype(F32)).astype(BF16)
        begin(z_first[mask])
    factor_sibling.wait_recv()
    begin(factor_y)
    own[lo, :, a, :] = own[lo, :, a, :] + recv1[0, lo].astype(F32)
    own[:, hi, b, :] = own[:, hi, b, :] + recv1[1, :, hi].astype(F32)

    y_first.wait_recv()
    for mask in z_masks:
        there = partner(hi, mask)
        z_send_last[mask - 1] = (own[lo, there, a, :] + y_recv_first[there].astype(F32)).astype(BF16)
        begin(z_last[mask])
    factor_y.wait_recv()
    for copy in factor_z:
        begin(copy)
    for mask in reversed(z_masks):
        z_first[mask].wait_recv()
    total = own[1 - lo, hi, b, :]
    for mask in z_masks:
        total += z_recv_first[mask - 1, 1 - lo].astype(F32)
    y_send_last[...] = total.astype(BF16)
    begin(y_last)
    total_a = own[lo, hi, a, :] + y_recv_first[hi].astype(F32)
    total_b = own[lo, hi, b, :]
    for mask in z_masks:
        total_b += z_recv_first[mask - 1, lo].astype(F32)
    for copy in factor_z:
        copy.wait_recv()
    for d in range(n):
        factor[d * own_rows : (d + 1) * own_rows, :] = factor_slots[d]
    for mask in reversed(z_masks):
        z_last[mask].wait_recv()
        total_a += z_recv_last[mask - 1].astype(F32)
    core_block[a, :] = total_a.astype(BF16)
    y_last.wait_recv()
    core_block[b, :] = (total_b + y_recv_last[...].astype(F32)).astype(BF16)

    panel = core_block[...]
    gram = lax.dot_general(
        panel, panel, (((1,), (1,)), ((), ())), preferred_element_type=F32
    ) * (1.0 / (ranks_two * ranks_three))
    top = gram.astype(BF16)
    rest = gram - top.astype(F32)
    middle = rest.astype(BF16)
    low = (rest - middle.astype(F32)).astype(BF16)
    stacked = jnp.concatenate([top, middle, low], axis=0)
    product = jnp.dot(stacked, factor[...].astype(BF16), preferred_element_type=F32)
    update[...] = (
        product[:subjects] + (product[subjects : 2 * subjects] + product[2 * subjects :])
    )
    for d in range(n):
        update_send[d] = update[d * own_rows : (d + 1) * own_rows, :]
    for copy in update_copies:
        begin(copy)
    total = update_send[me]
    for copy in reversed(update_copies):
        copy.wait_recv()
    for mask in range(1, n):
        total += update_recv[mask - 1]
    out_ref[...] = total
    for copy in sends:
        copy.wait_send()


def body(shape_data, frame_factor, coord_factor, subject_factor):
    n = lax.axis_size("coord")
    subjects, frames, width = shape_data.shape
    ranks_two = frame_factor.shape[1]
    ranks_three = coord_factor.shape[1]
    own_rows, ranks_one = subject_factor.shape
    nhi = n // 4
    rows = subjects // CHUNKS
    cols = ranks_two * ranks_three // n
    dma = pltpu.SemaphoreType.DMA
    return pl.pallas_call(
        functools.partial(kernel, n),
        out_shape=jax.ShapeDtypeStruct((own_rows, ranks_one), F32),
        in_specs=[pl.BlockSpec(memory_space=pl.ANY)] * 4,
        out_specs=pl.BlockSpec(memory_space=pltpu.VMEM),
        scratch_shapes=[
            pltpu.VMEM((frames, subjects, width), BF16),
            pltpu.VMEM((ranks_two, frames), BF16),
            pltpu.VMEM(coord_factor.shape, BF16),
            pltpu.VMEM(subject_factor.shape, BF16),
            pltpu.VMEM((2, nhi, subjects, cols), F32),
            pltpu.VMEM((CHUNKS, 2, nhi, rows, cols), BF16),
            pltpu.VMEM((CHUNKS, 2, nhi, rows, cols), BF16),
            pltpu.VMEM((nhi, rows, cols), BF16),
            pltpu.VMEM((nhi, rows, cols), BF16),
            pltpu.VMEM((nhi - 1, 2, rows, cols), BF16),
            pltpu.VMEM((nhi - 1, 2, rows, cols), BF16),
            pltpu.VMEM((rows, cols), BF16),
            pltpu.VMEM((rows, cols), BF16),
            pltpu.VMEM((nhi - 1, rows, cols), BF16),
            pltpu.VMEM((nhi - 1, rows, cols), BF16),
            pltpu.VMEM((subjects, cols), BF16),
            pltpu.VMEM((n, own_rows, ranks_one), F32),
            pltpu.VMEM((subjects, ranks_one), F32),
            pltpu.VMEM((subjects, ranks_one), F32),
            pltpu.VMEM((n, own_rows, ranks_one), F32),
            pltpu.VMEM((n - 1, own_rows, ranks_one), F32),
            dma((LOADS,)),
            dma((3,)),
            dma((CHUNKS,)),
            dma((CHUNKS,)),
            dma((2,)),
            dma((2,)),
            dma((2, nhi - 1)),
            dma((2, nhi - 1)),
            dma((1 + nhi,)),
            dma((1 + nhi,)),
            dma((n - 1,)),
            dma((n - 1,)),
        ],
        compiler_params=pltpu.CompilerParams(
            collective_id=0, has_side_effects=True, vmem_limit_bytes=60 * 1024 * 1024
        ),
    )(jnp.transpose(shape_data, (1, 0, 2)), frame_factor.T, coord_factor, subject_factor)


def solution(mesh):
    in_specs = (
        P("parts", None, "coord"),
        P("parts", None),
        P(("parts", "coord"), None),
        P(("parts", "coord"), None),
    )
    out_specs = P(("parts", "coord"), None)
    return jax.shard_map(body, mesh=mesh, in_specs=in_specs, out_specs=out_specs, check_vma=False)
```
